768 devices in a mesh: row: 24 (over z_hi, y), col: 32 (over x, z_lo, core).
Axes of the slice: x: 4, y: 8, z: 12 (z_hi: 3, z_lo: 4; z = z_hi * 4 + z_lo), core: 2. Of those that a mesh axis runs over, the one named last changes fastest.
Arguments:
- activations: bfloat16 [3072, 28672], P('row', 'col'), may hold values from -6 to 6
- gradients: bfloat16 [3072, 6144], P('col', 'row'), may hold values from -0.29882812 to 0.29882812
- seq_example: int32 [6], replicated, may hold values from 0 to 2, as said below
Outputs:
- eigen_corr: float32 [6144, 28672], P('row', 'col')
The draws below stay inside these ranges and needn't reach their ends.
Inputs may be any that keep to these rules, and one draw needn't show every extreme that they name: `seq_example`: every one of the 3 examples owns at least one of the 6 sequences.
All inputs are finite; a program needn't handle non-finite values.
Results may differ from the reference program's by a relative error of at most 0.0003.
Values may be sent and summed in bfloat16 or wider, within the bound.
A program may use at most 32 MiB of HBM per device.

```python
import jax
import jax.numpy as jnp
from jax import lax

INW = 28672
OUTW = 6144
SEQLEN = 512
SEQS = 6
EXAMPLES = 3
TOKENS = 3072
N_COL = 32


def draw_seq_example(key, part):
    key = jax.random.fold_in(key, 11)
    rest_key = jax.random.fold_in(key, 1)
    order_key = jax.random.fold_in(key, 2)
    covered = jnp.arange(EXAMPLES, dtype=jnp.int32)
    others = jax.random.randint(rest_key, (SEQS - EXAMPLES,), 0, EXAMPLES, dtype=jnp.int32)
    joined = jnp.concatenate([covered, others])
    return jax.random.permutation(order_key, joined)


def levels(own_key, dims, shards, smallest, high):
    def one(position, shards_of):
        heights = jax.random.uniform(jax.random.fold_in(jax.random.fold_in(own_key, 6), position), (shards_of,), jnp.float32, smallest / len(shards), high / len(shards))
        return jnp.repeat(jnp.exp(heights), dims[position] // shards_of).reshape((-1,) + (1,) * (len(dims) - position - 1))

    loudness = one(*shards[0])
    for cut in shards[1:]:
        loudness = loudness * one(*cut)
    return loudness


def scatter_about(rng, extent, deviation, reach, shards=(), kind=jnp.bfloat16):
    values = deviation * jax.random.normal(rng, extent, jnp.float32)
    if shards:
        values = values * levels(rng, extent, shards, -0.22, 0.18)
    return jnp.clip(values, -reach, reach).astype(kind)


def setup_inputs(seed: int = 0) -> dict:
    key_of = jax.random.split(jax.random.key(seed), 4)
    return {
        "activations": scatter_about(key_of[0], (TOKENS, INW), 1.0, 6.0, ((0, 24), (1, 32))),
        "gradients": scatter_about(key_of[1], (TOKENS, OUTW), 0.0442, 0.29882812, ((0, 32), (1, 24))),
        "seq_example": draw_seq_example(jax.random.fold_in(key_of[3], 71), 0),
    }


def reference(activations, gradients, seq_example):
    block = INW // N_COL
    grads_seq = gradients.astype(jnp.float32).reshape(SEQS, SEQLEN, OUTW)
    member = (seq_example[None, :] == jnp.arange(EXAMPLES, dtype=jnp.int32)[:, None]).astype(jnp.float32)
    acts_blocks = activations.reshape(TOKENS, N_COL, block).transpose(1, 0, 2)

    def one_block(acts_block):
        acts_seq = acts_block.astype(jnp.float32).reshape(SEQS, SEQLEN, block)
        seq_grad = jnp.einsum("sto,stc->soc", grads_seq, acts_seq, precision=lax.Precision.HIGHEST)
        example_grad = jnp.einsum("ns,soc->noc", member, seq_grad, precision=lax.Precision.HIGHEST)
        return jnp.sum(example_grad * example_grad, axis=0) / EXAMPLES

    result = lax.map(one_block, acts_blocks)
    return result.transpose(1, 0, 2).reshape(OUTW, INW)
```

```python
import jax
import jax.numpy as jnp
from jax import lax
from jax.experimental import pallas as pl
from jax.experimental.pallas import tpu as pltpu
from jax.sharding import PartitionSpec as P

MESH = pl.DeviceIdType.MESH
SEQLEN = 512
SEQS = 6
EXAMPLES = 3
TOKENS = 3072
NX, NY, NZH, NZL = 4, 8, 3, 4
BLK = TOKENS // (NY * NZH)
GBLK = TOKENS // (NX * NZL * 2)
WIDE = 256
NWIDE = 3
LAST = 128
HALF = BLK // 2
OUT_TILE = 256
IN_TILE = 896
UNITS = [(0, 0), (0, 1), (0, 2), (1, 0), (2, 0), (1, 1), (2, 1), (1, 2), (2, 2)]
START = {0: 0, 1: 0, 2: 0, 3: 3, 4: 3, 5: 4, 6: 4, 7: 5, 8: 5}


def body(seq_ref, acts_ref, grads_ref, out_ref, abuf, gmine, gall, obuf,
         loc_sem, out_sem, az_s, az_r, ay_s, ay_r, bz_s, bz_r, by_s, by_r, g1_s, g1_r, g2_s, g2_r, g3_s, g3_r):
    row, col = lax.axis_index("row"), lax.axis_index("col")
    zh, y = row // NY, row % NY
    x, zl, core = col // (2 * NZL), (col // 2) % NZL, col % 2

    def at_y(d):
        return (zh * NY + (y + d + NY) % NY, col)

    def at_z(d):
        return (((zh + d) % NZH) * NY + y, col)

    def at_zl(d):
        return (row, x * (2 * NZL) + ((zl + d) % NZL) * 2 + core)

    def at_x(d):
        return (row, ((x + d) % NX) * (2 * NZL) + zl * 2 + core)

    other = (row, col + 1 - 2 * core)
    peers = [at_y(1), at_y(-1), at_z(1), at_z(2)] + [at_zl(d) for d in (1, 2, 3)] + [at_x(d) for d in (1, 2, 3)] + [other]

    def tok(dz, dy, half=None):
        start = (((zh + dz) % NZH) * NY + (y + dy + NY) % NY) * BLK
        if half is None:
            return pl.ds(pl.multiple_of(start, BLK), BLK)
        return pl.ds(pl.multiple_of(start + half * HALF, HALF), HALF)

    def cols(j):
        return pl.ds(j * WIDE, WIDE if j < NWIDE else LAST)

    def copy(ref, src, ssem, rsem, to):
        return pltpu.make_async_remote_copy(
            src_ref=ref.at[src], dst_ref=ref.at[src], send_sem=ssem, recv_sem=rsem, device_id=to, device_id_type=MESH
        )

    sent = []

    def send(*args):
        c = copy(*args)
        c.start()
        sent.append(c)

    own_a = pltpu.make_async_copy(acts_ref, abuf.at[tok(0, 0), :], loc_sem.at[0])
    own_a.start()
    gslot = (x * NZL + zl) * GBLK

    def gtok(x_of, zl_of, n=1):
        return pl.ds(pl.multiple_of((x_of * NZL + zl_of) * GBLK, GBLK), n * GBLK)

    own_g = pltpu.make_async_copy(grads_ref, gmine.at[gtok(x, zl), :], loc_sem.at[1])
    own_g.start()
    barrier = pltpu.get_barrier_semaphore()
    for peer in peers:
        pl.semaphore_signal(barrier, inc=1, device_id=peer, device_id_type=MESH)
    pl.semaphore_wait(barrier, len(peers))
    own_g.wait()
    own_a.wait()

    def ring(ref, c, dz, h, way, ssem, rsem, go):
        step = 1 if way == 0 else -1
        half = None if h < 4 else way
        if go:
            send(ref, (tok(dz, -step * (h - 1), half), c), ssem, rsem, at_y(step))
        else:
            copy(ref, (tok(dz, -step * h, half), c), ssem, rsem, at_y(step)).wait_recv()

    def a_hop(u, h, go):
        dz, j = UNITS[u]
        for way in (0, 1):
            k = (u * 4 + h - 1) * 2 + way
            ring(abuf, cols(j), dz, h, way, ay_s.at[k], ay_r.at[k], go)

    def b_hop(h, go):
        for way in (0, 1):
            k = (h - 1) * 2 + way
            ring(abuf, cols(NWIDE), 0, h, way, by_s.at[k], by_r.at[k], go)

    def a_z_wait(u):
        dz, j = UNITS[u]
        k = j * 2 + dz - 1
        copy(abuf, (tok(dz, 0), cols(j)), az_s.at[k], az_r.at[k], at_z(dz)).wait_recv()

    def a_z_send(j):
        for d in (1, 2):
            k = j * 2 + (NZH - d) - 1
            send(abuf, (tok(0, 0), cols(j)), az_s.at[k], az_r.at[k], at_z(d))

    def b_z(dy, go):
        for d in (1, 2):
            dz = NZH - d
            k = (dy + 3) * 2 + dz - 1
            if go:
                send(abuf, (tok(0, dy), cols(NWIDE)), bz_s.at[k], bz_r.at[k], at_z(d))
            else:
                copy(abuf, (tok(dz, dy), cols(NWIDE)), bz_s.at[k], bz_r.at[k], at_z(d)).wait_recv()

    def g1(d, go):
        if go:
            send(gmine, (gtok(x, zl), slice(None)), g1_s.at[d - 1], g1_r.at[d - 1], at_zl(d))
        else:
            src = (gtok(x, (zl - d + NZL) % NZL), slice(None))
            copy(gmine, src, g1_s.at[d - 1], g1_r.at[d - 1], at_zl(d)).wait_recv()

    def g2(d, go):
        if go:
            send(gmine, (gtok(x, 0, NZL), slice(None)), g2_s.at[d - 1], g2_r.at[d - 1], at_x(d))
        else:
            src = (gtok((x - d + NX) % NX, 0, NZL), slice(None))
            copy(gmine, src, g2_s.at[d - 1], g2_r.at[d - 1], at_x(d)).wait_recv()

    gother = gall.at[1, pl.ds(0, TOKENS // 2), :]
    g3 = pltpu.make_async_remote_copy(
        src_ref=gmine, dst_ref=gother, send_sem=g3_s, recv_sem=g3_r, device_id=other, device_id_type=MESH
    )

    member = [[jnp.where(seq_ref[s] == n, 1.0, 0.0).astype(jnp.float32) for s in range(SEQS)] for n in range(EXAMPLES)]
    outs = []

    def compute(j):
        c = cols(j)
        totals = [None] * EXAMPLES
        for s in range(SEQS):
            part = lax.dot_general(
                gfull[s * SEQLEN:(s + 1) * SEQLEN, :],
                abuf[s * SEQLEN:(s + 1) * SEQLEN, c],
                (((0,), (0,)), ((), ())),
                preferred_element_type=jnp.float32,
            )
            for n in range(EXAMPLES):
                term = member[n][s] * part
                totals[n] = term if s == 0 else totals[n] + term
        total = sum(t * t for t in totals)
        obuf[:, c] = total / EXAMPLES
        out = pltpu.make_async_copy(obuf.at[:, c], out_ref.at[:, c], out_sem.at[j])
        out.start()
        outs.append(out)

    gfull = gall.at[0]
    last_wave = max(START.values()) + 4
    for w in range(last_wave):
        for u in range(len(UNITS)):
            h = w - START[u] + 1
            if h < 1 or h > 4:
                continue
            if h == 1 and UNITS[u][0] != 0:
                a_z_wait(u)
            if h > 1:
                a_hop(u, h - 1, False)
            a_hop(u, h, True)
        if w == 0:
            for d in (1, 2, 3):
                g1(d, True)
            for j in range(NWIDE):
                a_z_send(j)
            b_hop(1, True)
        if w == 1:
            for d in (1, 2, 3):
                g1(d, False)
            for d in (1, 2, 3):
                g2(d, True)
        if w in (1, 2, 3):
            b_hop(w, False)
            b_hop(w + 1, True)
        if w == 3:
            for d in (1, 2, 3):
                g2(d, False)
            g3.start()
        if w == 4:
            b_hop(4, False)
            b_z(0, True)
            b_z(1, True)
            b_z(-1, True)
        if w == 5:
            for dy in (2, -2, 3):
                b_z(dy, True)
            g3.wait_recv()
            for b in range(NX * NZL):
                mine = gmine[b * GBLK:(b + 1) * GBLK, :]
                theirs = gother[b * GBLK:(b + 1) * GBLK, :]
                first = jnp.where(core == 0, mine, theirs)
                second = jnp.where(core == 0, theirs, mine)
                gfull[2 * b * GBLK:(2 * b + 1) * GBLK, :] = first
                gfull[(2 * b + 1) * GBLK:(2 * b + 2) * GBLK, :] = second
        if w == 6:
            for dy in (-3, 4):
                b_z(dy, True)
        for j in range(NWIDE - 1):
            if w == START[UNITS.index((2, j))] + 4:
                for u, (dz, jj) in enumerate(UNITS):
                    if jj == j:
                        a_hop(u, 4, False)
                compute(j)
    for dy in (0, 1, -1, 2, -2, 3, -3, 4):
        b_z(dy, False)
    compute(NWIDE)
    for u, (dz, jj) in enumerate(UNITS):
        if jj == NWIDE - 1:
            a_hop(u, 4, False)
    compute(NWIDE - 1)
    for c in sent:
        c.wait_send()
    g3.wait_send()
    for out in outs:
        out.wait()


def on_device(activations, gradients, seq_example):
    dma = pltpu.SemaphoreType.DMA
    nu = len(UNITS)
    return pl.pallas_call(
        body,
        out_shape=jax.ShapeDtypeStruct((OUT_TILE, IN_TILE), jnp.float32),
        in_specs=[
            pl.BlockSpec(memory_space=pltpu.SMEM),
            pl.BlockSpec(memory_space=pl.ANY),
            pl.BlockSpec(memory_space=pl.ANY),
        ],
        out_specs=pl.BlockSpec(memory_space=pl.ANY),
        scratch_shapes=[
            pltpu.VMEM((TOKENS, IN_TILE), jnp.bfloat16),
            pltpu.VMEM((TOKENS // 2, OUT_TILE), jnp.bfloat16),
            pltpu.VMEM((2, TOKENS, OUT_TILE), jnp.bfloat16),
            pltpu.VMEM((OUT_TILE, IN_TILE), jnp.float32),
            dma((2,)),
            dma((NWIDE + 1,)),
            dma((2 * NWIDE,)),
            dma((2 * NWIDE,)),
            dma((nu * 8,)),
            dma((nu * 8,)),
            dma((16,)),
            dma((16,)),
            dma((8,)),
            dma((8,)),
            dma((3,)),
            dma((3,)),
            dma((3,)),
            dma((3,)),
            dma,
            dma,
        ],
        compiler_params=pltpu.CompilerParams(collective_id=0, has_side_effects=True, vmem_limit_bytes=40 << 20),
        cost_estimate=pl.CostEstimate(
            flops=2 * TOKENS * OUT_TILE * IN_TILE, bytes_accessed=OUT_TILE * IN_TILE * 4, transcendentals=0
        ),
        name="gather_and_correct",
    )(seq_example, activations, gradients)


def solution(mesh):
    placed = (P("row", "col"), P("col", "row"), P())
    return jax.shard_map(
        on_device, mesh=mesh, in_specs=placed, out_specs=P("row", "col"), check_vma=False
    )
```

```python
import jax
import jax.numpy as jnp
from jax import lax
from jax.experimental import pallas as pl
from jax.experimental.pallas import tpu as pltpu
from jax.sharding import PartitionSpec as P

MESH = pl.DeviceIdType.MESH
SEQLEN = 512
SEQS = 6
EXAMPLES = 3
TOKENS = 3072
NX, NY, NZH, NZL = 4, 8, 3, 4
BLK = TOKENS // (NY * NZH)
GBLK = TOKENS // (NX * NZL * 2)
NR = 2
PART = BLK // NR
OUT_TILE = 256
IN_TILE = 896
FIRST = (768,) * NR
UNITS = [(b, r) for b in range(NZH) for r in range(NR)]
CHUNKS = [(0, 256), (256, 256), (512, 256), (768, 128)]
START = {(b, r): 0.01 * r if b == 0 else 1.6 + 1.5 * b + 0.5 * r for b, r in UNITS}
Z_DOWN = [0.2 + 0.01 * r for r in range(NR)]
Z_LATE = [1.1, 2.05]
LATE = [0, 3]
Z_UP = [1.5 + 0.01 * r for r in range(NR)]
G1_DOWN, G1_UP, G2_WHEN, G3_WHEN, ORDER_WHEN = 0.15, 1.05, 4.6, 6.05, 7.5
SPREAD = [(4.4, (0, 1, -1)), (5.4, (2, -2, 3)), (6.4, (-3, 4))]
OWN_WHEN = 7.65
SECOND_WHEN = 8.2


def body(seq_ref, acts_ref, grads_ref, out_ref, abuf, gmine, gother, gfull, sums, obuf,
         loc_sem, out_sem, az_s, az_r, ay_s, ay_r, bz_s, bz_r, g1_s, g1_r, g2_s, g2_r, g3_s, g3_r, hi_sem, lo_sem, x_sem, core_sem):
    row, col = lax.axis_index("row"), lax.axis_index("col")
    zh, y = row // NY, row % NY
    x, zl, core = col // (2 * NZL), (col // 2) % NZL, col % 2
    planes = [zh, jnp.where(zh == 0, 1, 0), jnp.where(zh == 2, 1, 2)]

    def at_y(d):
        return (zh * NY + (y + d + NY) % NY, col)

    def at_z(b):
        return (planes[b] * NY + y, col)

    def at_zl(d):
        return (row, x * (2 * NZL) + ((zl + d) % NZL) * 2 + core)

    def at_x(d):
        return (row, ((x + d) % NX) * (2 * NZL) + zl * 2 + core)

    other = (row, col + 1 - 2 * core)

    def tok(b, dy, r=None):
        start = (planes[b] * NY + (y + dy + NY) % NY) * BLK
        if r is None:
            return pl.ds(pl.multiple_of(start, BLK), BLK)
        return pl.ds(pl.multiple_of(start + r * PART, PART), PART)

    def gtok(x_of, zl_of, n=1):
        return pl.ds(pl.multiple_of((x_of * NZL + zl_of) * GBLK, GBLK), n * GBLK)

    own_a = pltpu.make_async_copy(acts_ref, abuf.at[tok(0, 0), :], loc_sem.at[0])
    own_a.start()
    own_g = pltpu.make_async_copy(grads_ref, gmine.at[gtok(x, zl), :], loc_sem.at[1])
    own_g.start()

    corner = (x == 0) & (y == 0) & (core == 0)

    def rank(z):
        return jnp.where(corner & (z == 0), NZH * NZL, z)

    mine = rank(zh * NZL + zl)
    later_z = [None] + [rank(planes[b] * NZL + zl) > mine for b in (1, 2)]
    later_zl = [None] + [rank(zh * NZL + (zl + d) % NZL) > mine for d in (1, 2, 3)]
    later_x = [None] + [(x + d) % NX < x for d in (1, 2, 3)]
    pairs = [(later_z[b], at_z(b), hi_sem.at[zh]) for b in (1, 2)]
    pairs += [(later_zl[d], at_zl(d), lo_sem.at[zl]) for d in (1, 2, 3)]
    pairs += [(later_x[d], at_x(d), x_sem.at[x]) for d in (1, 2, 3)]
    pairs += [(core == 1, other, core_sem)]

    barrier = pltpu.get_barrier_semaphore()
    for peer in (at_y(1), at_y(-1)):
        pl.semaphore_signal(barrier, inc=1, device_id=peer, device_id_type=MESH)
    before_me = 2
    for later, peer, _ in pairs:
        before_me += jnp.where(later, 0, 1)

        @pl.when(later)
        def _():
            pl.semaphore_signal(barrier, inc=1, device_id=peer, device_id_type=MESH)
    pl.semaphore_wait(barrier, before_me)
    for later, peer, sem in pairs:
        @pl.when(jnp.logical_not(later))
        def _():
            pl.semaphore_signal(sem, inc=1, device_id=peer, device_id_type=MESH)
    own_a.wait()
    own_g.wait()

    def copy(ref, src, ssem, rsem, to):
        return pltpu.make_async_remote_copy(
            src_ref=ref.at[src], dst_ref=ref.at[src], send_sem=ssem, recv_sem=rsem, device_id=to, device_id_type=MESH
        )

    sent = []

    def send(*args):
        c = copy(*args)
        c.start()
        sent.append(c)

    def width(u):
        b, r = UNITS[u]
        return slice(None) if b == 0 else pl.ds(0, FIRST[r])

    def hop(u, way, h, go):
        b, r = UNITS[u]
        step = 1 if way == 0 else -1
        k = (u * 2 + way) * 4 + h - 1
        at = tok(b, -step * (h - 1 if go else h), r), width(u)
        if go:
            send(abuf, at, ay_s.at[k], ay_r.at[k], at_y(step))
        else:
            copy(abuf, at, ay_s.at[k], ay_r.at[k], at_y(step)).wait_recv()

    def last_hop(u, way):
        b, r = UNITS[u]
        return 4 if (r + b) % 2 == way else 3

    def y_step(u, h):
        b, r = UNITS[u]
        if h == 1 and b > 0:
            z_copy(r, b, b).wait_recv()
        for way in (0, 1):
            if 1 < h <= last_hop(u, way) + 1:
                hop(u, way, h - 1, False)
            if h <= last_hop(u, way):
                hop(u, way, h, True)

    def their(b):
        return jnp.where(zh > 3 - zh - planes[b], 2, 1)

    def z_copy(r, plane, number):
        k = (number - 1) * NR + r
        return copy(abuf, (tok(plane, 0, r), pl.ds(0, FIRST[r])), az_s.at[k], az_r.at[k], at_z(max(plane, 1)))

    def z_out(r, b):
        return pltpu.make_async_remote_copy(
            src_ref=abuf.at[tok(0, 0, r), pl.ds(0, FIRST[r])],
            dst_ref=abuf.at[tok(0, 0, r), pl.ds(0, FIRST[r])],
            send_sem=az_s.at[(b - 1) * NR + r],
            recv_sem=az_r.at[(their(b) - 1) * NR + r],
            device_id=at_z(b),
            device_id_type=MESH,
        )

    def z_up(r):
        for b in (1, 2):
            @pl.when(later_z[b])
            def _():
                if r == 0:
                    pl.semaphore_wait(hi_sem.at[planes[b]], 1)
                z_out(r, b).start()

    def z_down(r, first):
        for b in (1, 2):
            late = (planes[b] == (zh + 2) % NZH) & (zl < LATE[r])

            @pl.when(jnp.logical_not(later_z[b]) & (jnp.logical_not(late) if first else late))
            def _():
                z_out(r, b).start()

    def rest(dy, go):
        for b in (1, 2):
            for r in range(NR):
                if FIRST[r] == IN_TILE:
                    continue
                c = pl.ds(FIRST[r], IN_TILE - FIRST[r])
                k = (dy + 3) * 2 * NR + r
                if go:
                    send(abuf, (tok(0, dy, r), c), bz_s.at[k + NR * (b - 1)], bz_r.at[k + NR * (their(b) - 1)], at_z(b))
                else:
                    copy(abuf, (tok(b, dy, r), c), bz_s.at[k + NR * (b - 1)], bz_r.at[k + NR * (b - 1)], at_z(b)).wait_recv()

    def spread(*dys):
        for dy in dys:
            rest(dy, True)

    def g1_copy(d):
        return copy(gmine, (gtok(x, zl), slice(None)), g1_s.at[d - 1], g1_r.at[d - 1], at_zl(d))

    def g1_send(up):
        for d in (1, 2, 3):
            there = (zl + d) % NZL

            @pl.when(later_zl[d] if up else jnp.logical_not(later_zl[d]))
            def _():
                if up:
                    pl.semaphore_wait(lo_sem.at[there], 1)
                g1_copy(d).start()

    def g2_send():
        for d in (1, 2, 3):
            src = (gtok(x, (zl - d + NZL) % NZL), slice(None))
            copy(gmine, src, g1_s.at[d - 1], g1_r.at[d - 1], at_zl(d)).wait_recv()
        for d in (1, 2, 3):
            @pl.when(later_x[d])
            def _():
                pl.semaphore_wait(x_sem.at[(x + d) % NX], 1)
            send(gmine, (gtok(x, 0, NZL), slice(None)), g2_s.at[d - 1], g2_r.at[d - 1], at_x(d))

    g3 = pltpu.make_async_remote_copy(
        src_ref=gmine, dst_ref=gother, send_sem=g3_s, recv_sem=g3_r, device_id=other, device_id_type=MESH
    )

    def g3_send():
        for d in (1, 2, 3):
            src = (gtok((x - d + NX) % NX, 0, NZL), slice(None))
            copy(gmine, src, g2_s.at[d - 1], g2_r.at[d - 1], at_x(d)).wait_recv()

        @pl.when(core == 1)
        def _():
            pl.semaphore_wait(core_sem, 1)
        g3.start()

    def g_order():
        g3.wait_recv()
        for k in range(NX * NZL):
            ours = gmine[k * GBLK:(k + 1) * GBLK, :]
            theirs = gother[k * GBLK:(k + 1) * GBLK, :]
            gfull[2 * k * GBLK:(2 * k + 1) * GBLK, :] = jnp.where(core == 0, ours, theirs)
            gfull[(2 * k + 1) * GBLK:(2 * k + 2) * GBLK, :] = jnp.where(core == 0, theirs, ours)

    def seq_grad(b, i, c):
        at = pl.ds(pl.multiple_of((planes[b] * 2 + i) * SEQLEN, SEQLEN), SEQLEN)
        return lax.dot_general(
            gfull[at, :], abuf[at, c], (((0,), (0,)), ((), ())), preferred_element_type=jnp.float32
        )

    member = [
        [[jnp.where(seq_ref[planes[b] * 2 + i] == n, 1.0, 0.0) for i in (0, 1)] for b in range(NZH)]
        for n in range(EXAMPLES)
    ]

    def added(b, e, before, pair):
        for i in (0, 1):
            term = member[e][b][i] * pair[i]
            before = term if before is None else before + term
        return before

    def fold(b, chunks):
        for c0, n in chunks:
            c = pl.ds(c0, n)
            pair = [seq_grad(b, i, c) for i in (0, 1)]
            for e in range(EXAMPLES):
                sums[e, :, c] = added(b, e, None if b == 0 else sums[e, :, c], pair)

    events = [(START[UNITS[u]] + h - 1, y_step, u, h) for u in range(len(UNITS)) for h in (1, 2, 3, 4, 5)]
    events += [(when, z_down, r, True) for r, when in enumerate(Z_DOWN)]
    events += [(when, z_down, r, False) for r, when in enumerate(Z_LATE)]
    events += [(when, z_up, r) for r, when in enumerate(Z_UP)]
    events += [(when, spread, *dys) for when, dys in SPREAD]
    events += [(G1_DOWN, g1_send, False), (G1_UP, g1_send, True)]
    events += [(G2_WHEN, g2_send), (G3_WHEN, g3_send), (ORDER_WHEN, g_order), (OWN_WHEN, fold, 0, CHUNKS)]
    events += [(SECOND_WHEN, fold, 1, [c for c in CHUNKS if c[0] < min(FIRST)])]
    for _, what, *given in sorted(events, key=lambda e: e[0]):
        what(*given)
    for dy in range(-3, 5):
        rest(dy, False)

    outs = []
    for k, (c0, n) in enumerate(CHUNKS):
        c = pl.ds(c0, n)
        if c0 >= min(FIRST):
            fold(1, [(c0, n)])
        pair = [seq_grad(2, i, c) for i in (0, 1)]
        totals = [added(2, e, sums[e, :, c], pair) for e in range(EXAMPLES)]
        obuf[:, c] = sum(t * t for t in totals) / EXAMPLES
        out = pltpu.make_async_copy(obuf.at[:, c], out_ref.at[:, c], out_sem.at[k])
        out.start()
        outs.append(out)

    for b in (1, 2):
        for r in range(NR):
            z_out(r, b).wait_send()
    for d in (1, 2, 3):
        g1_copy(d).wait_send()
    for c in sent:
        c.wait_send()
    g3.wait_send()
    for out in outs:
        out.wait()


def on_device(activations, gradients, seq_example):
    dma, vmem = pltpu.SemaphoreType.DMA, pltpu.VMEM
    return pl.pallas_call(
        body,
        out_shape=jax.ShapeDtypeStruct((OUT_TILE, IN_TILE), jnp.float32),
        in_specs=[
            pl.BlockSpec(memory_space=pltpu.SMEM),
            pl.BlockSpec(memory_space=pl.ANY),
            pl.BlockSpec(memory_space=pl.ANY),
        ],
        out_specs=pl.BlockSpec(memory_space=pl.ANY),
        scratch_shapes=[
            vmem((TOKENS, IN_TILE), jnp.bfloat16),
            vmem((TOKENS // 2, OUT_TILE), jnp.bfloat16),
            vmem((TOKENS // 2, OUT_TILE), jnp.bfloat16),
            vmem((TOKENS, OUT_TILE), jnp.bfloat16),
            vmem((EXAMPLES, OUT_TILE, IN_TILE), jnp.float32),
            vmem((OUT_TILE, IN_TILE), jnp.float32),
            dma((2,)),
            dma((len(CHUNKS),)),
            dma((2 * NR,)),
            dma((2 * NR,)),
            dma((len(UNITS) * 8,)),
            dma((len(UNITS) * 8,)),
            dma((16 * NR,)),
            dma((16 * NR,)),
            dma((3,)),
            dma((3,)),
            dma((3,)),
            dma((3,)),
            dma,
            dma,
            pltpu.SemaphoreType.REGULAR((NZH,)),
            pltpu.SemaphoreType.REGULAR((NZL,)),
            pltpu.SemaphoreType.REGULAR((NX,)),
            pltpu.SemaphoreType.REGULAR,
        ],
        compiler_params=pltpu.CompilerParams(collective_id=0, has_side_effects=True, vmem_limit_bytes=58 << 20),
        cost_estimate=pl.CostEstimate(
            flops=2 * TOKENS * OUT_TILE * IN_TILE, bytes_accessed=OUT_TILE * IN_TILE * 4, transcendentals=0
        ),
        name="gather_and_correct",
    )(seq_example, activations, gradients)


def solution(mesh):
    placed = (P("row", "col"), P("col", "row"), P())
    return jax.shard_map(
        on_device, mesh=mesh, in_specs=placed, out_specs=P("row", "col"), check_vma=False
    )
```

```python
import jax
import jax.numpy as jnp
from jax import lax
from jax.experimental import pallas as pl
from jax.experimental.pallas import tpu as pltpu
from jax.sharding import PartitionSpec as P

MESH = pl.DeviceIdType.MESH
SEQLEN = 512
SEQS = 6
EXAMPLES = 3
TOKENS = 3072
NX, NY, NZH, NZL = 4, 8, 3, 4
BLK = TOKENS // (NY * NZH)
GBLK = TOKENS // (NX * NZL * 2)
NR = 2
PART = BLK // NR
OUT_TILE = 256
IN_TILE = 896
FIRST = 768
NREST = 2
REST_PART = NY * BLK // NREST
UNITS = [(b, r) for b in range(NZH) for r in range(NR)]
CHUNKS = [(0, 256), (256, 256), (512, 256), (768, 128)]
START = {(b, r): 0.01 * r if b == 0 else 1.6 + 1.5 * b + 0.9 * r for b, r in UNITS}
Z_DOWN = [0.2 + 0.01 * r for r in range(NR)]
Z_LATE = [1.1, 2.05]
LATE = [0, 3]
Z_UP = [1.5 + 0.01 * r for r in range(NR)]
G1_DOWN, G1_UP, G2_WHEN, G3_WHEN, ORDER_WHEN = 0.15, 1.05, 4.6, 6.05, 7.5
SPREAD = 4.15
OWN_WHEN = 7.65
SECOND_WHEN = 8.2


def body(seq_ref, acts_ref, grads_ref, out_ref, abuf, gmine, gother, gfull, sums, rest_own, rest_far, obuf,
         loc_sem, out_sem, az_s, az_r, ay_s, ay_r, bz_s, bz_r, g1_s, g1_r, g2_s, g2_r, g3_s, g3_r, hi_sem, lo_sem, x_sem, core_sem):
    row, col = lax.axis_index("row"), lax.axis_index("col")
    zh, y = row // NY, row % NY
    x, zl, core = col // (2 * NZL), (col // 2) % NZL, col % 2
    planes = [zh, jnp.where(zh == 0, 1, 0), jnp.where(zh == 2, 1, 2)]

    def at_y(d):
        return (zh * NY + (y + d + NY) % NY, col)

    def at_z(b):
        return (planes[b] * NY + y, col)

    def at_zl(d):
        return (row, x * (2 * NZL) + ((zl + d) % NZL) * 2 + core)

    def at_x(d):
        return (row, ((x + d) % NX) * (2 * NZL) + zl * 2 + core)

    other = (row, col + 1 - 2 * core)

    def tok(b, dy, r=None):
        start = (planes[b] * NY + (y + dy + NY) % NY) * BLK
        if r is None:
            return pl.ds(pl.multiple_of(start, BLK), BLK)
        return pl.ds(pl.multiple_of(start + r * PART, PART), PART)

    def gtok(x_of, zl_of, n=1):
        return pl.ds(pl.multiple_of((x_of * NZL + zl_of) * GBLK, GBLK), n * GBLK)

    own_a = pltpu.make_async_copy(acts_ref, abuf.at[tok(0, 0), :], loc_sem.at[0])
    own_a.start()
    own_g = pltpu.make_async_copy(grads_ref, gmine.at[gtok(x, zl), :], loc_sem.at[1])
    own_g.start()

    corner = (x == 0) & (y == 0) & (core == 0)

    def rank(z):
        return jnp.where(corner & (z == 0), NZH * NZL, z)

    mine = rank(zh * NZL + zl)
    later_z = [None] + [rank(planes[b] * NZL + zl) > mine for b in (1, 2)]
    later_zl = [None] + [rank(zh * NZL + (zl + d) % NZL) > mine for d in (1, 2, 3)]
    later_x = [None] + [(x + d) % NX < x for d in (1, 2, 3)]
    pairs = [(later_z[b], at_z(b), hi_sem.at[zh]) for b in (1, 2)]
    pairs += [(later_zl[d], at_zl(d), lo_sem.at[zl]) for d in (1, 2, 3)]
    pairs += [(later_x[d], at_x(d), x_sem.at[x]) for d in (1, 2, 3)]
    pairs += [(core == 1, other, core_sem)]

    barrier = pltpu.get_barrier_semaphore()
    for peer in (at_y(1), at_y(-1)):
        pl.semaphore_signal(barrier, inc=1, device_id=peer, device_id_type=MESH)
    before_me = 2
    for later, peer, _ in pairs:
        before_me += jnp.where(later, 0, 1)

        @pl.when(later)
        def _():
            pl.semaphore_signal(barrier, inc=1, device_id=peer, device_id_type=MESH)
    pl.semaphore_wait(barrier, before_me)
    for later, peer, sem in pairs:
        @pl.when(jnp.logical_not(later))
        def _():
            pl.semaphore_signal(sem, inc=1, device_id=peer, device_id_type=MESH)
    own_a.wait()
    own_g.wait()

    def copy(ref, src, ssem, rsem, to):
        return pltpu.make_async_remote_copy(
            src_ref=ref.at[src], dst_ref=ref.at[src], send_sem=ssem, recv_sem=rsem, device_id=to, device_id_type=MESH
        )

    sent = []

    def send(*args):
        c = copy(*args)
        c.start()
        sent.append(c)

    def width(u):
        b, r = UNITS[u]
        return slice(None) if b == 0 else pl.ds(0, FIRST)

    def hop(u, way, h, go):
        b, r = UNITS[u]
        step = 1 if way == 0 else -1
        k = (u * 2 + way) * 4 + h - 1
        at = tok(b, -step * (h - 1 if go else h), r), width(u)
        if go:
            send(abuf, at, ay_s.at[k], ay_r.at[k], at_y(step))
        else:
            copy(abuf, at, ay_s.at[k], ay_r.at[k], at_y(step)).wait_recv()

    def last_hop(u, way):
        b, r = UNITS[u]
        return 4 if (r + b) % 2 == way else 3

    def y_step(u, h):
        b, r = UNITS[u]
        if h == 1 and b > 0:
            z_copy(r, b, b).wait_recv()
        for way in (0, 1):
            if 1 < h <= last_hop(u, way) + 1:
                hop(u, way, h - 1, False)
            if h <= last_hop(u, way):
                hop(u, way, h, True)

    def their(b):
        return jnp.where(zh > 3 - zh - planes[b], 2, 1)

    def z_copy(r, plane, number):
        k = (number - 1) * NR + r
        return copy(abuf, (tok(plane, 0, r), pl.ds(0, FIRST)), az_s.at[k], az_r.at[k], at_z(max(plane, 1)))

    def z_out(r, b):
        return pltpu.make_async_remote_copy(
            src_ref=abuf.at[tok(0, 0, r), pl.ds(0, FIRST)],
            dst_ref=abuf.at[tok(0, 0, r), pl.ds(0, FIRST)],
            send_sem=az_s.at[(b - 1) * NR + r],
            recv_sem=az_r.at[(their(b) - 1) * NR + r],
            device_id=at_z(b),
            device_id_type=MESH,
        )

    def z_up(r):
        for b in (1, 2):
            @pl.when(later_z[b])
            def _():
                if r == 0:
                    pl.semaphore_wait(hi_sem.at[planes[b]], 1)
                z_out(r, b).start()

    def z_down(r, first):
        for b in (1, 2):
            late = (planes[b] == (zh + 2) % NZH) & (zl < LATE[r])

            @pl.when(jnp.logical_not(later_z[b]) & (jnp.logical_not(late) if first else late))
            def _():
                z_out(r, b).start()

    def rest(b, p):
        at = pl.ds(p * REST_PART, REST_PART)
        return pltpu.make_async_remote_copy(
            src_ref=rest_own.at[at],
            dst_ref=rest_far.at[their(b) - 1, at],
            send_sem=bz_s.at[(b - 1) * NREST + p],
            recv_sem=bz_r.at[(their(b) - 1) * NREST + p],
            device_id=at_z(b),
            device_id_type=MESH,
        )

    def spread():
        rest_own[...] = abuf[pl.ds(pl.multiple_of(zh * (NY * BLK), NY * BLK), NY * BLK), FIRST:IN_TILE]
        for p in range(NREST):
            for b in (1, 2):
                rest(b, p).start()

    def rest_wait(b, p):
        at = pl.ds(p * REST_PART, REST_PART)
        pltpu.make_async_remote_copy(
            src_ref=rest_own.at[at],
            dst_ref=rest_far.at[b - 1, at],
            send_sem=bz_s.at[(b - 1) * NREST + p],
            recv_sem=bz_r.at[(b - 1) * NREST + p],
            device_id=at_z(b),
            device_id_type=MESH,
        ).wait_recv()

    def g1_copy(d):
        return copy(gmine, (gtok(x, zl), slice(None)), g1_s.at[d - 1], g1_r.at[d - 1], at_zl(d))

    def g1_send(up):
        for d in (1, 2, 3):
            there = (zl + d) % NZL

            @pl.when(later_zl[d] if up else jnp.logical_not(later_zl[d]))
            def _():
                if up:
                    pl.semaphore_wait(lo_sem.at[there], 1)
                g1_copy(d).start()

    def g2_send():
        for d in (1, 2, 3):
            src = (gtok(x, (zl - d + NZL) % NZL), slice(None))
            copy(gmine, src, g1_s.at[d - 1], g1_r.at[d - 1], at_zl(d)).wait_recv()
        for d in (1, 2, 3):
            @pl.when(later_x[d])
            def _():
                pl.semaphore_wait(x_sem.at[(x + d) % NX], 1)
            send(gmine, (gtok(x, 0, NZL), slice(None)), g2_s.at[d - 1], g2_r.at[d - 1], at_x(d))

    g3 = pltpu.make_async_remote_copy(
        src_ref=gmine, dst_ref=gother, send_sem=g3_s, recv_sem=g3_r, device_id=other, device_id_type=MESH
    )

    def g3_send():
        for d in (1, 2, 3):
            src = (gtok((x - d + NX) % NX, 0, NZL), slice(None))
            copy(gmine, src, g2_s.at[d - 1], g2_r.at[d - 1], at_x(d)).wait_recv()

        @pl.when(core == 1)
        def _():
            pl.semaphore_wait(core_sem, 1)
        g3.start()

    def g_order():
        g3.wait_recv()
        for k in range(NX * NZL):
            ours = gmine[k * GBLK:(k + 1) * GBLK, :]
            theirs = gother[k * GBLK:(k + 1) * GBLK, :]
            gfull[2 * k * GBLK:(2 * k + 1) * GBLK, :] = jnp.where(core == 0, ours, theirs)
            gfull[(2 * k + 1) * GBLK:(2 * k + 2) * GBLK, :] = jnp.where(core == 0, theirs, ours)

    def seq_grad(b, i, c):
        at = pl.ds(pl.multiple_of((planes[b] * 2 + i) * SEQLEN, SEQLEN), SEQLEN)
        if b > 0 and c.start >= FIRST:
            acts = rest_far[b - 1, i * SEQLEN:(i + 1) * SEQLEN, c.start - FIRST:c.start - FIRST + c.size]
        else:
            acts = abuf[at, c]
        return lax.dot_general(
            gfull[at, :], acts, (((0,), (0,)), ((), ())), preferred_element_type=jnp.float32
        )

    member = [
        [[jnp.where(seq_ref[planes[b] * 2 + i] == n, 1.0, 0.0) for i in (0, 1)] for b in range(NZH)]
        for n in range(EXAMPLES)
    ]

    def added(b, e, before, pair):
        for i in (0, 1):
            term = member[e][b][i] * pair[i]
            before = term if before is None else before + term
        return before

    def fold(b, chunks):
        for c0, n in chunks:
            c = pl.ds(c0, n)
            pair = [seq_grad(b, i, c) for i in (0, 1)]
            for e in range(EXAMPLES):
                sums[e, :, c] = added(b, e, None if b == 0 else sums[e, :, c], pair)

    events = [(START[UNITS[u]] + h - 1, y_step, u, h) for u in range(len(UNITS)) for h in (1, 2, 3, 4, 5)]
    events += [(when, z_down, r, True) for r, when in enumerate(Z_DOWN)]
    events += [(when, z_down, r, False) for r, when in enumerate(Z_LATE)]
    events += [(when, z_up, r) for r, when in enumerate(Z_UP)]
    events += [(SPREAD, spread)]
    events += [(G1_DOWN, g1_send, False), (G1_UP, g1_send, True)]
    events += [(G2_WHEN, g2_send), (G3_WHEN, g3_send), (ORDER_WHEN, g_order), (OWN_WHEN, fold, 0, CHUNKS)]
    events += [(SECOND_WHEN, fold, 1, [c for c in CHUNKS if c[0] < FIRST])]
    for _, what, *given in sorted(events, key=lambda e: e[0]):
        what(*given)
    for b in (1, 2):
        for p in range(NREST):
            rest_wait(b, p)

    outs = []
    for k, (c0, n) in enumerate(CHUNKS):
        c = pl.ds(c0, n)
        if c0 >= FIRST:
            fold(1, [(c0, n)])
        pair = [seq_grad(2, i, c) for i in (0, 1)]
        totals = [added(2, e, sums[e, :, c], pair) for e in range(EXAMPLES)]
        obuf[:, c] = sum(t * t for t in totals) / EXAMPLES
        out = pltpu.make_async_copy(obuf.at[:, c], out_ref.at[:, c], out_sem.at[k])
        out.start()
        outs.append(out)

    for b in (1, 2):
        for r in range(NR):
            z_out(r, b).wait_send()
        for p in range(NREST):
            rest(b, p).wait_send()
    for d in (1, 2, 3):
        g1_copy(d).wait_send()
    for c in sent:
        c.wait_send()
    g3.wait_send()
    for out in outs:
        out.wait()


def on_device(activations, gradients, seq_example):
    dma, vmem = pltpu.SemaphoreType.DMA, pltpu.VMEM
    return pl.pallas_call(
        body,
        out_shape=jax.ShapeDtypeStruct((OUT_TILE, IN_TILE), jnp.float32),
        in_specs=[
            pl.BlockSpec(memory_space=pltpu.SMEM),
            pl.BlockSpec(memory_space=pl.ANY),
            pl.BlockSpec(memory_space=pl.ANY),
        ],
        out_specs=pl.BlockSpec(memory_space=pl.ANY),
        scratch_shapes=[
            vmem((TOKENS, IN_TILE), jnp.bfloat16),
            vmem((TOKENS // 2, OUT_TILE), jnp.bfloat16),
            vmem((TOKENS // 2, OUT_TILE), jnp.bfloat16),
            vmem((TOKENS, OUT_TILE), jnp.bfloat16),
            vmem((EXAMPLES, OUT_TILE, IN_TILE), jnp.float32),
            vmem((NY * BLK, IN_TILE - FIRST), jnp.bfloat16),
            vmem((2, NY * BLK, IN_TILE - FIRST), jnp.bfloat16),
            vmem((OUT_TILE, IN_TILE), jnp.float32),
            dma((2,)),
            dma((len(CHUNKS),)),
            dma((2 * NR,)),
            dma((2 * NR,)),
            dma((len(UNITS) * 8,)),
            dma((len(UNITS) * 8,)),
            dma((2 * NREST,)),
            dma((2 * NREST,)),
            dma((3,)),
            dma((3,)),
            dma((3,)),
            dma((3,)),
            dma,
            dma,
            pltpu.SemaphoreType.REGULAR((NZH,)),
            pltpu.SemaphoreType.REGULAR((NZL,)),
            pltpu.SemaphoreType.REGULAR((NX,)),
            pltpu.SemaphoreType.REGULAR,
        ],
        compiler_params=pltpu.CompilerParams(collective_id=0, has_side_effects=True, vmem_limit_bytes=58 << 20),
        cost_estimate=pl.CostEstimate(
            flops=2 * TOKENS * OUT_TILE * IN_TILE, bytes_accessed=OUT_TILE * IN_TILE * 4, transcendentals=0
        ),
        name="gather_and_correct",
    )(seq_example, activations, gradients)


def solution(mesh):
    placed = (P("row", "col"), P("col", "row"), P())
    return jax.shard_map(
        on_device, mesh=mesh, in_specs=placed, out_specs=P("row", "col"), check_vma=False
    )
```
